32 devices in a mesh: group: 2 (over x), space: 16 (over z, y, core).
Axes of the slice: x: 2, y: 2, z: 4, core: 2. Of those that a mesh axis runs over, the one named last changes fastest.
Arguments:
- columns_in: bfloat16 [8192, 1024], P(('group', 'space')), parts along dimension 0, may hold values from -6 to 6
- cotangent: bfloat16 [8192, 1024], P(('group', 'space')), parts along dimension 0, may hold values from -6 to 6
- conv_weight: bfloat16 [7, 16, 16], replicated, may hold values from -0.5 to 0.5
- mix_weight: bfloat16 [1024, 1024], replicated, may hold values from -0.1875 to 0.1875
- neighbours: int32 [4096, 7], P('space'), may hold values from 0 to 4095, as said below
- rotations: int32 [4096], P('space'), may hold values from 0 to 5
- pentagons: int32 [4096], P('space'), may hold values 0 or 1
Outputs:
- grad_input: bfloat16 [8192, 1024], P(('group', 'space')), parts along dimension 0
- grad_mix: float32 [1024, 2048], P('space', 'group'), parts along dimension 1
- grad_conv: float32 [14, 16, 16], P('group'), parts along dimension 0
The draws below stay inside these ranges and needn't reach their ends.
There are 2 independent parts, one for each index of `group`. The reference program is written for one: setup_inputs(seed, part) draws one part's arguments, and reference() takes and returns one part's arrays. A program takes and returns all parts, laid end to end along the dimension named above; an argument that names none is the same for every part. Nothing has to cross between parts.
Inputs may be any that keep to these rules, and one draw needn't show every extreme that they name: `neighbours`: entry 0 of each row is the column itself. Every other entry lies in the column's own grid row of 256 consecutive column indices or in the row just before or after it, the last row of the grid followed by the first. The relation is symmetric: if b is a neighbour of a, then a is a neighbour of b.
All inputs are finite; a program needn't handle non-finite values. No bound on the sum of `pentagons` on one device may be relied on, other than what follows from the above.
Results may differ from the reference program's by a relative error of at most 0.005.
Values may be sent and summed in bfloat16 or wider, within the bound.
A program may use at most 128 MiB of HBM per device.

```python
import jax
import jax.numpy as jnp

C = 16
LEV = 64
F = 1024
TAPS = 7
ROW = 256
COLS = 4096


def draw_neighbours(key, part):
    grid_rows = COLS // ROW
    shears = jax.random.randint(key, (grid_rows,), 0, ROW, dtype=jnp.int32)
    column_ids = jnp.arange(COLS, dtype=jnp.int32)
    row_ids = column_ids // ROW
    place = column_ids % ROW
    above = (row_ids + 1) % grid_rows
    below = (row_ids - 1 + grid_rows) % grid_rows
    shear_here = shears[row_ids]
    shear_below = shears[below]

    def locate(row_index, place_index):
        return row_index * ROW + place_index % ROW
    return jnp.stack([column_ids, locate(row_ids, place + 1), locate(above, place + shear_here), locate(above, place + shear_here - 1), locate(row_ids, place - 1), locate(below, place - shear_below), locate(below, place - shear_below + 1)], axis=1).astype(jnp.int32)


def with_ends(entries, stream_key, smallest, largest):
    longest = entries.shape.index(max(entries.shape))
    spots = []
    for shift in (0, 1):
        where = [jax.random.randint(jax.random.fold_in(stream_key, axis), (), 0, length) for axis, length in enumerate(entries.shape)]
        where[longest] = (where[longest] + shift) % entries.shape[longest]
        spots.append(tuple(where))
    return entries.at[spots[0]].set(smallest).at[spots[1]].set(largest)


def with_spikes(drawn, own_key, source, target, blocks, factor):
    owner, partner = [(jnp.arange(drawn.shape[axis_at]) // (drawn.shape[axis_at] // blocks)).reshape([-1 if axis == axis_at else 1 for axis in range(drawn.ndim)]) for axis_at in (source, target)]
    chosen = jax.random.permutation(own_key, blocks)[partner]
    strong = (owner == chosen) | (owner == (partner + blocks // 2) % blocks)
    return jnp.where(strong, factor * drawn, drawn)


def levels(own_key, extent, shards, low, top_value):
    gain = 1.0
    for position, shards_of in shards:
        draws = jax.random.uniform(jax.random.fold_in(jax.random.fold_in(own_key, 6), position), (shards_of,), jnp.float32, low / len(shards), top_value / len(shards))
        gain = gain * jnp.repeat(jnp.exp(draws), extent[position] // shards_of).reshape((-1,) + (1,) * (len(extent) - 1 - position))
    return gain


def centred(rng, extent, width, most, shards=(), held_as=jnp.bfloat16):
    factor_of = levels(rng, extent, shards, -0.22, 0.18) if shards else 1.0
    entries = jax.random.normal(rng, extent, jnp.float32) * width * factor_of
    return jnp.minimum(jnp.maximum(entries, -most), most).astype(held_as)


def gaussian_with(stream_key, shape, scale, most, shards, heavy, kind=jnp.bfloat16):
    values = scale * jax.random.normal(stream_key, shape, jnp.float32)
    if shards:
        values = values * levels(stream_key, shape, shards, -0.22, 0.18)
    return jnp.clip(with_spikes(values, jax.random.fold_in(stream_key, 3), *heavy), -most, most).astype(kind)


def setup_inputs(seed: int = 0, part: int = 0) -> dict:
    splits = jax.random.split(jax.random.key(seed), 8)
    part_splits = jax.random.split(jax.random.fold_in(splits[7], part), 8)
    return {
        "columns_in": gaussian_with(part_splits[0], (COLS, F), 1.0, 6.0, ((0, 16),), (0, 1, 16, 2.0)),
        "cotangent": centred(part_splits[1], (COLS, F), 1.0, 6.0, ((0, 16),)),
        "conv_weight": centred(splits[2], (TAPS, C, C), (TAPS * C) ** -0.5, 0.5),
        "mix_weight": centred(splits[3], (F, F), F ** -0.5, 0.1875),
        "neighbours": draw_neighbours(jax.random.fold_in(splits[7], 71), part),
        "rotations": with_ends(jax.random.randint(splits[5], (COLS,), 0, 6), jax.random.fold_in(splits[5], 1), 0, 5).astype(jnp.int32),
        "pentagons": with_ends((jax.random.randint(splits[6], (COLS,), 0, 16) < 1).astype(jnp.int32), jax.random.fold_in(splits[6], 1), 0, 1),
    }


def tap_sources(neighbours, rotations, pentagons, index_tap):
    if index_tap == 0:
        slot_index = jnp.zeros_like(rotations)
    else:
        slot_index = 1 + (index_tap - 1 - rotations) % 6
    source = jnp.take_along_axis(neighbours, slot_index[:, None], axis=1)[:, 0]
    keep_mask = 1 - pentagons * (slot_index == 6).astype(jnp.int32)
    return (source, keep_mask)

def reference(columns_in, cotangent, conv_weight, mix_weight, neighbours, rotations, pentagons):
    preact = jnp.zeros((COLS, LEV, C), jnp.float32)
    for index_tap in range(TAPS):
        source, keep_mask = tap_sources(neighbours, rotations, pentagons, index_tap)
        tap_rows = jnp.take(columns_in, source, axis=0) * keep_mask.astype(jnp.bfloat16)[:, None]
        preact = preact + jnp.einsum('nlc,cd->nld', tap_rows.reshape(COLS, LEV, C).astype(jnp.float32), conv_weight[index_tap].astype(jnp.float32))
    output, pullback = jax.vjp(jax.nn.gelu, preact)
    active = output.reshape(COLS, F).astype(jnp.bfloat16)
    upstream = jnp.dot(cotangent, mix_weight.T, preferred_element_type=jnp.float32)
    grad_pre = pullback(upstream.reshape(COLS, LEV, C))[0].astype(jnp.bfloat16)
    grad_mix = jnp.dot(active.T, cotangent, preferred_element_type=jnp.float32) / jnp.sqrt(jnp.float32(COLS))
    spread = cotangent.astype(jnp.float32)
    conv_terms = []
    for index_tap in range(TAPS):
        source, keep_mask = tap_sources(neighbours, rotations, pentagons, index_tap)
        tap_rows = jnp.take(columns_in, source, axis=0) * keep_mask.astype(jnp.bfloat16)[:, None]
        conv_terms.append(jnp.einsum('nlc,nld->cd', tap_rows.reshape(COLS, LEV, C).astype(jnp.float32), grad_pre.astype(jnp.float32)))
        tap_term = jnp.einsum('nld,cd->nlc', grad_pre.astype(jnp.float32), conv_weight[index_tap].astype(jnp.float32)).reshape(COLS, F)
        tap_term = tap_term * keep_mask.astype(jnp.float32)[:, None]
        spread = spread + jax.ops.segment_sum(tap_term, source, num_segments=COLS)
    grad_conv = jnp.stack(conv_terms) / jnp.sqrt(jnp.float32(COLS * LEV))
    return (spread.astype(jnp.bfloat16), grad_mix, grad_conv)
```

```python
import functools

import jax
import jax.numpy as jnp
from jax import lax
from jax.experimental import pallas as pl
from jax.experimental.pallas import tpu as pltpu
from jax.sharding import PartitionSpec as P

ROW = 256
LANES = 256
F32 = jnp.float32
BF16 = jnp.bfloat16


def dot(a, b, dims=((1,), (0,)), precision=None):
    return lax.dot_general(a, b, (dims, ((), ())), preferred_element_type=F32, precision=precision)


def remote(src, dst, send, recv, target):
    return pltpu.make_async_remote_copy(
        src_ref=src,
        dst_ref=dst,
        send_sem=send,
        recv_sem=recv,
        device_id={"space": target},
        device_id_type=pl.DeviceIdType.MESH,
    )


def kernel(
    devices,
    x_ref, cot_ref, conv_ref, mix_ref, idx_ref, idx_t_ref,
    grad_ref, gmix_ref, gconv_ref,
    ext, hot, hot_t, wide, wide_t, ups, taps, gpre, terms, spread_mid, edges, edges_in,
    part, part_in, summed, summed_in, conv_acc, conv_own, conv_in,
    halo_send, halo_recv, edge_send, edge_recv, core_send, core_recv, chip_send, chip_recv,
    conv_send, conv_recv,
):
    tile, features = x_ref.shape
    taps_n, channels, _ = conv_ref.shape
    blocks = features // LANES
    share = features // devices
    chips = devices // 2
    owners = LANES // share
    me = lax.axis_index("space")
    nxt, prv = lax.rem(me + 1, devices), lax.rem(me + devices - 1, devices)
    core = lax.rem(me, 2)
    chip = me // 2
    twin = chip * 2 + (1 - core)

    barrier = pltpu.get_barrier_semaphore()

    @pl.loop(1, devices)
    def _(d):
        pl.semaphore_signal(
            barrier, inc=1, device_id={"space": lax.rem(me + d, devices)},
            device_id_type=pl.DeviceIdType.MESH,
        )

    pl.semaphore_wait(barrier, devices - 1)

    to_next = remote(x_ref, ext.at[pl.ds(0, ROW)], halo_send.at[0], halo_recv.at[0], nxt)
    to_prev = remote(x_ref, ext.at[pl.ds(ROW + tile, ROW)], halo_send.at[1], halo_recv.at[1], prv)
    to_next.start()
    to_prev.start()

    ext[ROW : ROW + tile, :] = x_ref[...]
    width = tile + 2 * ROW
    lane_ids = lax.broadcasted_iota(jnp.int32, (tile, width), 1)
    row_ids = lax.broadcasted_iota(jnp.int32, (width, tile), 0)
    for j in range(1, taps_n):
        hot[(j - 1) * tile : j * tile, :] = (lane_ids == idx_ref[:, j : j + 1]).astype(F32).astype(BF16)
        hot_t[:, (j - 1) * tile : j * tile] = (row_ids == idx_t_ref[j : j + 1, :]).astype(F32).astype(BF16)
    spot = lax.broadcasted_iota(jnp.int32, (LANES, channels), 0) % channels
    pick = (spot == lax.broadcasted_iota(jnp.int32, (LANES, channels), 1)).astype(F32).astype(BF16)
    same = (
        lax.broadcasted_iota(jnp.int32, (LANES, LANES), 0) // channels
        == lax.broadcasted_iota(jnp.int32, (LANES, LANES), 1) // channels
    )
    for j in range(taps_n):
        w = conv_ref[j]
        full = dot(dot(pick, w).astype(BF16), pick, ((1,), (1,)))
        wide[j * LANES : (j + 1) * LANES, :] = jnp.where(same, full, 0.0).astype(BF16)
        full_t = dot(dot(pick, w, ((1,), (1,))).astype(BF16), pick, ((1,), (1,)))
        wide_t[:, j * LANES : (j + 1) * LANES] = jnp.where(same, full_t, 0.0).astype(BF16)

    @pl.loop(0, blocks)
    def _(k):
        rows = pl.ds(pl.multiple_of(k * LANES, LANES), LANES)
        ups[k] = dot(cot_ref[...], mix_ref[rows, :], ((1,), (1,)))

    to_next.wait()
    to_prev.wait()

    def core_copy(k):
        per = owners // 2
        at = pl.ds(k * per, per)
        return remote(
            part.at[1 - core, at], part_in.at[at], core_send.at[k], core_recv.at[k], twin
        )

    @pl.loop(0, blocks)
    def _(k):
        cols = pl.ds(pl.multiple_of(k * LANES, LANES), LANES)
        source = ext[:, cols]
        taps[k, :, 0:LANES] = ext[ROW : ROW + tile, cols]
        for j in range(1, taps_n):
            taps[k, :, j * LANES : (j + 1) * LANES] = dot(
                hot[(j - 1) * tile : j * tile, :], source
            ).astype(BF16)
        pre = dot(taps[k], wide[...])
        square = pre * pre
        scale = 0.7978845608028654
        t = jnp.tanh(scale * pre * (1.0 + 0.044715 * square))
        half = 0.5 * (1.0 + t)
        active = (pre * half).astype(BF16)
        slope = half + 0.5 * pre * (1.0 - t * t) * scale * (1.0 + 3 * 0.044715 * square)
        gpre[k] = (ups[k] * slope).astype(BF16)
        local = dot(active, cot_ref[...], ((0,), (0,))).astype(BF16)
        for i in range(owners):
            part[i % 2, k * (owners // 2) + i // 2] = local[i * share : (i + 1) * share, :]
        core_copy(k).start()

    def chip_copy(d):
        target = lax.rem(chip + d, chips)
        return remote(
            summed.at[target], summed_in.at[d], chip_send.at[d], chip_recv.at[d],
            target * 2 + core,
        )

    @pl.loop(0, blocks)
    def _(k):
        core_copy(k).wait()

    @pl.loop(0, chips)
    def _(h):
        summed[h] = (part[core, h].astype(F32) + part_in[h].astype(F32)).astype(BF16)

    @pl.loop(1, chips)
    def _(d):
        chip_copy(d).start()

    @pl.loop(0, blocks)
    def _(k):
        cols = pl.ds(pl.multiple_of(k * LANES, LANES), LANES)
        g = gpre[k]
        own = dot(g, wide_t[:, 0:LANES]) + cot_ref[:, cols].astype(F32)
        for j in range(1, taps_n):
            terms[(j - 1) * tile : j * tile, :] = dot(
                g, wide_t[:, j * LANES : (j + 1) * LANES]
            ).astype(BF16)
        edges[0, :, cols] = dot(hot_t[0:ROW, :], terms[...]).astype(BF16)
        spread_mid[:, cols] = own + dot(hot_t[ROW : ROW + tile, :], terms[...])
        edges[1, :, cols] = dot(hot_t[ROW + tile :, :], terms[...]).astype(BF16)

    edge_prev = remote(edges.at[0], edges_in.at[0], edge_send.at[0], edge_recv.at[0], prv)
    edge_next = remote(edges.at[1], edges_in.at[1], edge_send.at[1], edge_recv.at[1], nxt)
    edge_prev.start()
    edge_next.start()

    conv_acc[...] = jnp.zeros_like(conv_acc)

    @pl.loop(0, blocks)
    def _(k):
        conv_acc[...] += dot(gpre[k], taps[k], ((0,), (0,)))

    rows_same = lax.broadcasted_iota(jnp.int32, (LANES, LANES), 0) // channels
    cols_same = lax.broadcasted_iota(jnp.int32, (LANES, LANES), 1) // channels
    out_lane = lax.broadcasted_iota(jnp.int32, (LANES, 128), 1)
    in_place = lax.broadcasted_iota(jnp.int32, (LANES, 128), 0) % channels
    total = jnp.zeros((channels, 128), F32)
    for j in range(taps_n):
        block = jnp.where(rows_same == cols_same, conv_acc[:, j * LANES : (j + 1) * LANES], 0.0)
        folded = block[0:channels, :]
        for l in range(1, LANES // channels):
            folded = folded + block[l * channels : (l + 1) * channels, :]
        place = (out_lane == in_place + j * channels).astype(F32)
        total = total + dot(folded, place, precision=lax.Precision.HIGHEST)
    conv_own[...] = total

    def conv_copy(d):
        return remote(
            conv_own, conv_in.at[d], conv_send.at[d], conv_recv.at[d], lax.rem(me + d, devices)
        )

    @pl.loop(1, devices)
    def _(d):
        conv_copy(d).start()

    edge_prev.wait()
    edge_next.wait()
    first, last = edges_in[1].astype(F32), edges_in[0].astype(F32)
    if tile == ROW:
        grad_ref[...] = (spread_mid[...] + first + last).astype(BF16)
    else:
        spread_mid[0:ROW, :] += first
        spread_mid[tile - ROW :, :] += last
        grad_ref[...] = spread_mid[...].astype(BF16)

    conv_in[0] = conv_own[...]

    @pl.loop(1, devices)
    def _(d):
        conv_copy(d).wait()

    def add_conv(owner, acc):
        return acc + conv_in[lax.rem(me - owner + devices, devices)]

    gconv_ref[...] = lax.fori_loop(0, devices, add_conv, jnp.zeros((channels, 128), F32)) * (
        1.0 / (devices * tile * (features // channels)) ** 0.5
    )

    gmix_ref[...] = part[core, chip].astype(F32) + part_in[chip].astype(F32)

    @pl.loop(1, chips)
    def _(d):
        chip_copy(d).wait()
        gmix_ref[...] += summed_in[d].astype(F32)

    gmix_ref[...] = gmix_ref[...] * (1.0 / (devices * tile) ** 0.5)


def shards(columns_in, cotangent, conv_weight, mix_weight, neighbours, rotations, pentagons):
    tile, features = columns_in.shape
    taps_n, channels, _ = conv_weight.shape
    devices = lax.axis_size("space")
    total_cols = tile * devices
    offset = lax.axis_index("space") * tile
    share = features // devices
    chips = devices // 2
    blocks = features // LANES
    width = tile + 2 * ROW

    taps_at = lax.broadcasted_iota(jnp.int32, (8, tile), 0)
    slot = jnp.where(taps_at == 0, 0, 1 + (taps_at - 1 - rotations[None, :]) % 6)
    near = (neighbours.T - offset + ROW) % total_cols
    source = jnp.zeros((8, tile), jnp.int32)
    for s in range(taps_n):
        source = jnp.where(slot == s, near[s : s + 1, :], source)
    index_t = jnp.where((slot == 6) & (pentagons[None, :] != 0), -1, source)
    index = index_t.T

    vmem = pl.BlockSpec(memory_space=pltpu.VMEM)
    grad_input, grad_mix, conv = pl.pallas_call(
        functools.partial(kernel, devices),
        out_shape=(
            jax.ShapeDtypeStruct((tile, features), BF16),
            jax.ShapeDtypeStruct((share, features), F32),
            jax.ShapeDtypeStruct((channels, 128), F32),
        ),
        in_specs=[vmem] * 6,
        out_specs=(vmem,) * 3,
        scratch_shapes=[
            pltpu.VMEM((width, features), BF16),
            pltpu.VMEM(((taps_n - 1) * tile, width), BF16),
            pltpu.VMEM((width, (taps_n - 1) * tile), BF16),
            pltpu.VMEM((taps_n * LANES, LANES), BF16),
            pltpu.VMEM((LANES, taps_n * LANES), BF16),
            pltpu.VMEM((blocks, tile, LANES), F32),
            pltpu.VMEM((blocks, tile, taps_n * LANES), BF16),
            pltpu.VMEM((blocks, tile, LANES), BF16),
            pltpu.VMEM(((taps_n - 1) * tile, LANES), BF16),
            pltpu.VMEM((tile, features), F32),
            pltpu.VMEM((2, ROW, features), BF16),
            pltpu.VMEM((2, ROW, features), BF16),
            pltpu.VMEM((2, chips, share, features), BF16),
            pltpu.VMEM((chips, share, features), BF16),
            pltpu.VMEM((chips, share, features), BF16),
            pltpu.VMEM((chips, share, features), BF16),
            pltpu.VMEM((LANES, taps_n * LANES), F32),
            pltpu.VMEM((channels, 128), F32),
            pltpu.VMEM((devices, channels, 128), F32),
            pltpu.SemaphoreType.DMA((2,)),
            pltpu.SemaphoreType.DMA((2,)),
            pltpu.SemaphoreType.DMA((2,)),
            pltpu.SemaphoreType.DMA((2,)),
            pltpu.SemaphoreType.DMA((blocks,)),
            pltpu.SemaphoreType.DMA((blocks,)),
            pltpu.SemaphoreType.DMA((chips,)),
            pltpu.SemaphoreType.DMA((chips,)),
            pltpu.SemaphoreType.DMA((devices,)),
            pltpu.SemaphoreType.DMA((devices,)),
        ],
        compiler_params=pltpu.CompilerParams(
            collective_id=0, has_side_effects=True, vmem_limit_bytes=52 * 1024 * 1024
        ),
    )(columns_in, cotangent, conv_weight, mix_weight, index, index_t)
    grad_conv = conv.reshape(channels, 128 // channels, channels)[:, :taps_n].transpose(1, 2, 0)
    return grad_input, grad_mix, grad_conv


def solution(mesh):
    return jax.shard_map(
        shards,
        mesh=mesh,
        in_specs=(
            P(("group", "space"), None),
            P(("group", "space"), None),
            P(),
            P(),
            P("space", None),
            P("space"),
            P("space"),
        ),
        out_specs=(P(("group", "space"), None), P("space", "group"), P("group", None, None)),
        check_vma=False,
    )
```

```python
import functools

import jax
import jax.numpy as jnp
from jax import lax
from jax.experimental import pallas as pl
from jax.experimental.pallas import tpu as pltpu
from jax.sharding import PartitionSpec as P

ROW = 256
LANES = 256
F32 = jnp.float32
BF16 = jnp.bfloat16


def dot(a, b, dims=((1,), (0,)), precision=None):
    return lax.dot_general(a, b, (dims, ((), ())), preferred_element_type=F32, precision=precision)


def remote(src, dst, send, recv, target):
    return pltpu.make_async_remote_copy(
        src_ref=src,
        dst_ref=dst,
        send_sem=send,
        recv_sem=recv,
        device_id={"space": target},
        device_id_type=pl.DeviceIdType.MESH,
    )


def kernel(
    devices,
    x_ref, cot_hbm, conv_hbm, mix_hbm, near_hbm, rot_hbm, pent_hbm,
    grad_ref, gmix_ref, gconv_ref,
    cot_ref, conv_ref, mix_ref, near_ref, rot_ref, pent_ref, index_pad,
    ext, hot, hot_t, wide, wide_t, ups, taps, gpre, terms, spread_mid, edges, edges_in,
    part, part_in, summed, summed_in, conv_acc, conv_own, conv_in,
    load_sem, mid_sem, halo_send, halo_recv, edge_send, edge_recv, core_send, core_recv,
    chip_send, chip_recv, conv_send, conv_recv,
):
    tile, features = x_ref.shape
    taps_n, channels, _ = conv_ref.shape
    blocks = features // LANES
    share = features // devices
    chips = devices // 2
    owners = LANES // share
    total_cols = tile * devices
    width = tile + 2 * ROW
    me = lax.axis_index("space")
    nxt, prv = lax.rem(me + 1, devices), lax.rem(me + devices - 1, devices)
    core = lax.rem(me, 2)
    chip = me // 2
    twin = chip * 2 + (1 - core)

    barrier = pltpu.get_barrier_semaphore()

    @pl.loop(1, devices)
    def _(d):
        pl.semaphore_signal(
            barrier, inc=1, device_id={"space": lax.rem(me + d, devices)},
            device_id_type=pl.DeviceIdType.MESH,
        )

    loads = [
        pltpu.make_async_copy(source, target, load_sem.at[n])
        for n, (source, target) in enumerate([
            (near_hbm, near_ref), (rot_hbm, rot_ref), (pent_hbm, pent_ref),
            (conv_hbm, conv_ref), (cot_hbm, cot_ref), (mix_hbm, mix_ref),
        ])
    ]
    for load in loads:
        load.start()

    def lanes(k):
        return pl.ds(pl.multiple_of(k * LANES, LANES), LANES)

    def block_at(i, device):
        return lax.rem(i + 1 + device // owners, blocks)

    def mid_copy(k):
        return pltpu.make_async_copy(
            x_ref.at[:, lanes(k)], ext.at[k, pl.ds(ROW, tile)], mid_sem.at[k]
        )

    def halo_next(k):
        return remote(
            x_ref.at[pl.ds(tile - ROW, ROW), lanes(k)], ext.at[k, pl.ds(0, ROW)],
            halo_send.at[0, k], halo_recv.at[0, k], nxt,
        )

    def halo_prev(k):
        return remote(
            x_ref.at[pl.ds(0, ROW), lanes(k)], ext.at[k, pl.ds(ROW + tile, ROW)],
            halo_send.at[1, k], halo_recv.at[1, k], prv,
        )

    def edge_prev(k):
        return remote(
            edges.at[0, k], edges_in.at[0, k], edge_send.at[0, k], edge_recv.at[0, k], prv
        )

    def edge_next(k):
        return remote(
            edges.at[1, k], edges_in.at[1, k], edge_send.at[1, k], edge_recv.at[1, k], nxt
        )

    @pl.loop(0, blocks)
    def _(i):
        mid_copy(block_at(i, me)).start()

    pl.semaphore_wait(barrier, devices - 1)

    @pl.loop(0, blocks)
    def _(i):
        halo_next(block_at(i, nxt)).start()
        halo_prev(block_at(i, prv)).start()

    for load in loads[:4]:
        load.wait()
    index_pad[...] = jnp.zeros_like(index_pad)
    away = near_ref[...] - me * tile
    away = jnp.where(away < 0, away + total_cols, away) + ROW
    away = jnp.where(away >= total_cols, away - total_cols, away)
    tap_ids = lax.broadcasted_iota(jnp.int32, (8, tile), 0)
    slot = tap_ids - 1 - jnp.broadcast_to(rot_ref[...], (8, tile))
    slot = jnp.where(tap_ids == 0, 0, 1 + jnp.where(slot < 0, slot + 6, slot))
    found = jnp.zeros((8, tile), jnp.int32)
    for n in range(taps_n):
        found = jnp.where(slot == n, jnp.broadcast_to(away[n : n + 1, :], (8, tile)), found)
    void = (slot == 6) & (jnp.broadcast_to(pent_ref[...], (8, tile)) != 0)
    found = jnp.where(void, -1, found)
    index_pad[0:8, :] = found
    index = index_pad[...].T

    spot = lax.broadcasted_iota(jnp.int32, (LANES, channels), 0) % channels
    pick = (spot == lax.broadcasted_iota(jnp.int32, (LANES, channels), 1)).astype(F32).astype(BF16)
    same = (
        lax.broadcasted_iota(jnp.int32, (LANES, LANES), 0) // channels
        == lax.broadcasted_iota(jnp.int32, (LANES, LANES), 1) // channels
    )
    for j in range(taps_n):
        w = conv_ref[j]
        full = dot(dot(pick, w).astype(BF16), pick, ((1,), (1,)))
        wide[j * LANES : (j + 1) * LANES, :] = jnp.where(same, full, 0.0).astype(BF16)
        full_t = dot(dot(pick, w, ((1,), (1,))).astype(BF16), pick, ((1,), (1,)))
        wide_t[:, j * LANES : (j + 1) * LANES] = jnp.where(same, full_t, 0.0).astype(BF16)
    lane_ids = lax.broadcasted_iota(jnp.int32, (tile, width), 1)
    row_ids = lax.broadcasted_iota(jnp.int32, (width, tile), 0)
    for j in range(1, taps_n):
        hot[(j - 1) * tile : j * tile, :] = (lane_ids == index[:, j : j + 1]).astype(F32).astype(BF16)
        hot_t[:, (j - 1) * tile : j * tile] = (row_ids == found[j : j + 1, :]).astype(F32).astype(BF16)

    for load in loads[4:]:
        load.wait()

    @pl.loop(0, blocks)
    def _(k):
        ups[k] = dot(cot_ref[...], mix_ref[lanes(k), :], ((1,), (1,)))

    conv_acc[...] = jnp.zeros_like(conv_acc)

    def core_copy(k):
        per = owners // 2
        at = pl.ds(k * per, per)
        return remote(
            part.at[1 - core, at], part_in.at[at], core_send.at[k], core_recv.at[k], twin
        )

    def chip_copy(target, d):
        return remote(
            summed.at[target], summed_in.at[d], chip_send.at[d], chip_recv.at[d],
            target * 2 + core,
        )

    def pass_on(k):
        core_copy(k).wait()

        @pl.loop(0, owners // 2)
        def _(n):
            h = k * (owners // 2) + n
            summed[h] = (part[core, h].astype(F32) + part_in[h].astype(F32)).astype(BF16)

            @pl.when(h != chip)
            def _():
                chip_copy(h, lax.rem(h - chip + chips, chips)).start()

    @pl.loop(0, blocks)
    def _(i):
        k = block_at(i, me)
        cols = lanes(k)
        mid_copy(k).wait()
        halo_next(k).wait_recv()
        halo_prev(k).wait_recv()
        source = ext[k]
        taps[k, :, 0:LANES] = ext[k, ROW : ROW + tile, :]
        for j in range(1, taps_n):
            taps[k, :, j * LANES : (j + 1) * LANES] = dot(
                hot[(j - 1) * tile : j * tile, :], source
            ).astype(BF16)
        pre = dot(taps[k], wide[...])
        square = pre * pre
        scale = 0.7978845608028654
        t = jnp.tanh(scale * pre * (1.0 + 0.044715 * square))
        half = 0.5 * (1.0 + t)
        active = (pre * half).astype(BF16)
        slope = half + 0.5 * pre * (1.0 - t * t) * scale * (1.0 + 3 * 0.044715 * square)
        gpre[k] = (ups[k] * slope).astype(BF16)
        local = dot(active, cot_ref[...], ((0,), (0,))).astype(BF16)
        for n in range(owners):
            part[n % 2, k * (owners // 2) + n // 2] = local[n * share : (n + 1) * share, :]
        core_copy(k).start()

        g = gpre[k]
        for j in range(1, taps_n):
            terms[(j - 1) * tile : j * tile, :] = dot(
                g, wide_t[:, j * LANES : (j + 1) * LANES]
            ).astype(BF16)
        edges[0, k] = dot(hot_t[0:ROW, :], terms[...]).astype(BF16)
        edge_prev(k).start()
        edges[1, k] = dot(hot_t[ROW + tile :, :], terms[...]).astype(BF16)
        edge_next(k).start()
        pass_on(k)
        own = dot(g, wide_t[:, 0:LANES]) + cot_ref[:, cols].astype(F32)
        spread_mid[k] = own + dot(hot_t[ROW : ROW + tile, :], terms[...])
        conv_acc[...] += dot(g, taps[k], ((0,), (0,)))

    rows_same = lax.broadcasted_iota(jnp.int32, (LANES, LANES), 0) // channels
    cols_same = lax.broadcasted_iota(jnp.int32, (LANES, LANES), 1) // channels
    out_lane = lax.broadcasted_iota(jnp.int32, (LANES, 128), 1)
    in_place = lax.broadcasted_iota(jnp.int32, (LANES, 128), 0) % channels
    total = jnp.zeros((channels, 128), F32)
    for j in range(taps_n):
        block = jnp.where(rows_same == cols_same, conv_acc[:, j * LANES : (j + 1) * LANES], 0.0)
        folded = block[0:channels, :]
        for l in range(1, LANES // channels):
            folded = folded + block[l * channels : (l + 1) * channels, :]
        place = (out_lane == in_place + j * channels).astype(F32)
        total = total + dot(folded, place, precision=lax.Precision.HIGHEST)
    conv_own[...] = total

    def conv_copy(d):
        return remote(
            conv_own, conv_in.at[d], conv_send.at[d], conv_recv.at[d], lax.rem(me + d, devices)
        )

    @pl.loop(1, devices)
    def _(d):
        conv_copy(d).start()

    @pl.loop(0, blocks)
    def _(i):
        k = block_at(i, me)
        edge_prev(k).wait_recv()
        edge_next(k).wait_recv()
        spread_mid[k, 0:ROW, :] += edges_in[1, k].astype(F32)
        spread_mid[k, tile - ROW :, :] += edges_in[0, k].astype(F32)
        grad_ref[:, lanes(k)] = spread_mid[k].astype(BF16)

    conv_in[0] = conv_own[...]

    @pl.loop(1, devices)
    def _(d):
        conv_copy(d).wait()

    def add_conv(owner, acc):
        return acc + conv_in[lax.rem(me - owner + devices, devices)]

    gconv_ref[...] = lax.fori_loop(0, devices, add_conv, jnp.zeros((channels, 128), F32)) * (
        1.0 / (devices * tile * (features // channels)) ** 0.5
    )

    gmix_ref[...] = part[core, chip].astype(F32) + part_in[chip].astype(F32)

    @pl.loop(1, chips)
    def _(d):
        chip_copy(lax.rem(chip + d, chips), d).wait()
        gmix_ref[...] += summed_in[d].astype(F32)

    gmix_ref[...] = gmix_ref[...] * (1.0 / (devices * tile) ** 0.5)

    @pl.loop(0, blocks)
    def _(k):
        halo_next(k).wait_send()
        halo_prev(k).wait_send()
        edge_prev(k).wait_send()
        edge_next(k).wait_send()


def shards(columns_in, cotangent, conv_weight, mix_weight, neighbours, rotations, pentagons):
    tile, features = columns_in.shape
    taps_n, channels, _ = conv_weight.shape
    devices = lax.axis_size("space")
    share = features // devices
    chips = devices // 2
    blocks = features // LANES
    width = tile + 2 * ROW

    vmem = pl.BlockSpec(memory_space=pltpu.VMEM)
    grad_input, grad_mix, conv = pl.pallas_call(
        functools.partial(kernel, devices),
        out_shape=(
            jax.ShapeDtypeStruct((tile, features), BF16),
            jax.ShapeDtypeStruct((share, features), F32),
            jax.ShapeDtypeStruct((channels, 128), F32),
        ),
        in_specs=[pl.BlockSpec(memory_space=pltpu.HBM)] * 7,
        out_specs=(vmem,) * 3,
        scratch_shapes=[
            pltpu.VMEM((tile, features), BF16),
            pltpu.VMEM((taps_n, channels, channels), BF16),
            pltpu.VMEM((features, features), BF16),
            pltpu.VMEM((taps_n, tile), jnp.int32),
            pltpu.VMEM((1, tile), jnp.int32),
            pltpu.VMEM((1, tile), jnp.int32),
            pltpu.VMEM((128, tile), jnp.int32),
            pltpu.VMEM((blocks, width, LANES), BF16),
            pltpu.VMEM(((taps_n - 1) * tile, width), BF16),
            pltpu.VMEM((width, (taps_n - 1) * tile), BF16),
            pltpu.VMEM((taps_n * LANES, LANES), BF16),
            pltpu.VMEM((LANES, taps_n * LANES), BF16),
            pltpu.VMEM((blocks, tile, LANES), F32),
            pltpu.VMEM((blocks, tile, taps_n * LANES), BF16),
            pltpu.VMEM((blocks, tile, LANES), BF16),
            pltpu.VMEM(((taps_n - 1) * tile, LANES), BF16),
            pltpu.VMEM((blocks, tile, LANES), F32),
            pltpu.VMEM((2, blocks, ROW, LANES), BF16),
            pltpu.VMEM((2, blocks, ROW, LANES), BF16),
            pltpu.VMEM((2, chips, share, features), BF16),
            pltpu.VMEM((chips, share, features), BF16),
            pltpu.VMEM((chips, share, features), BF16),
            pltpu.VMEM((chips, share, features), BF16),
            pltpu.VMEM((LANES, taps_n * LANES), F32),
            pltpu.VMEM((channels, 128), F32),
            pltpu.VMEM((devices, channels, 128), F32),
            pltpu.SemaphoreType.DMA((6,)),
            pltpu.SemaphoreType.DMA((blocks,)),
            pltpu.SemaphoreType.DMA((2, blocks)),
            pltpu.SemaphoreType.DMA((2, blocks)),
            pltpu.SemaphoreType.DMA((2, blocks)),
            pltpu.SemaphoreType.DMA((2, blocks)),
            pltpu.SemaphoreType.DMA((blocks,)),
            pltpu.SemaphoreType.DMA((blocks,)),
            pltpu.SemaphoreType.DMA((chips,)),
            pltpu.SemaphoreType.DMA((chips,)),
            pltpu.SemaphoreType.DMA((devices,)),
            pltpu.SemaphoreType.DMA((devices,)),
        ],
        compiler_params=pltpu.CompilerParams(
            collective_id=0, has_side_effects=True, vmem_limit_bytes=63 * 1024 * 1024
        ),
    )(
        columns_in, cotangent, conv_weight, mix_weight, neighbours.T,
        rotations.reshape(1, tile), pentagons.reshape(1, tile),
    )
    grad_conv = conv.reshape(channels, 128 // channels, channels)[:, :taps_n].transpose(1, 2, 0)
    return grad_input, grad_mix, grad_conv


def solution(mesh):
    return jax.shard_map(
        shards,
        mesh=mesh,
        in_specs=(
            P(("group", "space"), None),
            P(("group", "space"), None),
            P(),
            P(),
            P("space", None),
            P("space"),
            P("space"),
        ),
        out_specs=(P(("group", "space"), None), P("space", "group"), P("group", None, None)),
        check_vma=False,
    )
```

```python
import functools

import jax
import jax.numpy as jnp
from jax import lax
from jax.experimental import pallas as pl
from jax.experimental.pallas import tpu as pltpu
from jax.sharding import PartitionSpec as P

ROW = 256
LANES = 256
F32 = jnp.float32
BF16 = jnp.bfloat16


def dot(a, b, dims=((1,), (0,)), precision=None):
    return lax.dot_general(a, b, (dims, ((), ())), preferred_element_type=F32, precision=precision)


def remote(src, dst, send, recv, target):
    return pltpu.make_async_remote_copy(
        src_ref=src,
        dst_ref=dst,
        send_sem=send,
        recv_sem=recv,
        device_id={"space": target},
        device_id_type=pl.DeviceIdType.MESH,
    )


def kernel(
    devices,
    x_ref, cot_hbm, conv_hbm, mix_hbm, near_hbm, rot_hbm, pent_hbm,
    grad_ref, gmix_ref, gconv_ref,
    cot_ref, conv_ref, mix_ref, near_ref, rot_ref, pent_ref, index_pad,
    ext, hot, hot_t, wide, wide_t, ups, taps, gpre, terms, spread_mid, edges, edges_in,
    part, part_in, summed, pair_in, paired, summed_in, conv_acc, conv_own, conv_in,
    load_sem, mid_sem, halo_send, halo_recv, edge_send, edge_recv, core_send, core_recv,
    pair_send, pair_recv, chip_send, chip_recv, conv_send, conv_recv,
):
    tile, features = x_ref.shape
    taps_n, channels, _ = conv_ref.shape
    blocks = features // LANES
    share = features // devices
    chips = devices // 2
    owners = LANES // share
    total_cols = tile * devices
    width = tile + 2 * ROW
    me = lax.axis_index("space")
    nxt, prv = lax.rem(me + 1, devices), lax.rem(me + devices - 1, devices)
    core = lax.rem(me, 2)
    chip = me // 2
    twin = chip * 2 + (1 - core)

    barrier = pltpu.get_barrier_semaphore()

    @pl.loop(1, devices)
    def _(d):
        pl.semaphore_signal(
            barrier, inc=1, device_id={"space": lax.rem(me + d, devices)},
            device_id_type=pl.DeviceIdType.MESH,
        )

    loads = [
        pltpu.make_async_copy(source, target, load_sem.at[n])
        for n, (source, target) in enumerate([
            (near_hbm, near_ref), (rot_hbm, rot_ref), (pent_hbm, pent_ref),
            (conv_hbm, conv_ref), (cot_hbm, cot_ref), (mix_hbm, mix_ref),
        ])
    ]
    for load in loads:
        load.start()

    def lanes(k):
        return pl.ds(pl.multiple_of(k * LANES, LANES), LANES)

    def block_at(i, device):
        return lax.rem(i + 1 + device // owners, blocks)

    def mid_copy(k):
        return pltpu.make_async_copy(
            x_ref.at[:, lanes(k)], ext.at[k, pl.ds(ROW, tile)], mid_sem.at[k]
        )

    def halo_next(k):
        return remote(
            x_ref.at[pl.ds(tile - ROW, ROW), lanes(k)], ext.at[k, pl.ds(0, ROW)],
            halo_send.at[0, k], halo_recv.at[0, k], nxt,
        )

    def halo_prev(k):
        return remote(
            x_ref.at[pl.ds(0, ROW), lanes(k)], ext.at[k, pl.ds(ROW + tile, ROW)],
            halo_send.at[1, k], halo_recv.at[1, k], prv,
        )

    def edge_prev(k):
        return remote(
            edges.at[0, k], edges_in.at[0, k], edge_send.at[0, k], edge_recv.at[0, k], prv
        )

    def edge_next(k):
        return remote(
            edges.at[1, k], edges_in.at[1, k], edge_send.at[1, k], edge_recv.at[1, k], nxt
        )

    @pl.loop(0, blocks)
    def _(i):
        mid_copy(block_at(i, me)).start()

    pl.semaphore_wait(barrier, devices - 1)

    @pl.loop(0, blocks)
    def _(i):
        halo_next(block_at(i, nxt)).start()
        halo_prev(block_at(i, prv)).start()

    for load in loads[:4]:
        load.wait()
    index_pad[...] = jnp.zeros_like(index_pad)
    away = near_ref[...] - me * tile
    away = jnp.where(away < 0, away + total_cols, away) + ROW
    away = jnp.where(away >= total_cols, away - total_cols, away)
    tap_ids = lax.broadcasted_iota(jnp.int32, (8, tile), 0)
    slot = tap_ids - 1 - jnp.broadcast_to(rot_ref[...], (8, tile))
    slot = jnp.where(tap_ids == 0, 0, 1 + jnp.where(slot < 0, slot + 6, slot))
    found = jnp.zeros((8, tile), jnp.int32)
    for n in range(taps_n):
        found = jnp.where(slot == n, jnp.broadcast_to(away[n : n + 1, :], (8, tile)), found)
    void = (slot == 6) & (jnp.broadcast_to(pent_ref[...], (8, tile)) != 0)
    found = jnp.where(void, -1, found)
    index_pad[0:8, :] = found
    index = index_pad[...].T

    spot = lax.broadcasted_iota(jnp.int32, (LANES, channels), 0) % channels
    pick = (spot == lax.broadcasted_iota(jnp.int32, (LANES, channels), 1)).astype(F32).astype(BF16)
    same = (
        lax.broadcasted_iota(jnp.int32, (LANES, LANES), 0) // channels
        == lax.broadcasted_iota(jnp.int32, (LANES, LANES), 1) // channels
    )
    for j in range(taps_n):
        w = conv_ref[j]
        full = dot(dot(pick, w).astype(BF16), pick, ((1,), (1,)))
        wide[j * LANES : (j + 1) * LANES, :] = jnp.where(same, full, 0.0).astype(BF16)
        full_t = dot(dot(pick, w, ((1,), (1,))).astype(BF16), pick, ((1,), (1,)))
        wide_t[:, j * LANES : (j + 1) * LANES] = jnp.where(same, full_t, 0.0).astype(BF16)
    lane_ids = lax.broadcasted_iota(jnp.int32, (tile, width), 1)
    row_ids = lax.broadcasted_iota(jnp.int32, (width, tile), 0)
    for j in range(1, taps_n):
        hot[(j - 1) * tile : j * tile, :] = (lane_ids == index[:, j : j + 1]).astype(F32).astype(BF16)
        hot_t[:, (j - 1) * tile : j * tile] = (row_ids == found[j : j + 1, :]).astype(F32).astype(BF16)

    for load in loads[4:]:
        load.wait()

    @pl.loop(0, blocks)
    def _(k):
        ups[k] = dot(cot_ref[...], mix_ref[lanes(k), :], ((1,), (1,)))

    conv_acc[...] = jnp.zeros_like(conv_acc)

    def core_copy(k):
        per = owners // 2
        at = pl.ds(k * per, per)
        return remote(
            part.at[1 - core, at], part_in.at[at], core_send.at[k], core_recv.at[k], twin
        )

    half = owners // 4
    pairs = chips // 2
    parity = lax.rem(chip, 2)
    pair = chip // 2
    mate = (chip + 1 - 2 * parity) * 2 + core

    def pair_copy(k):
        at = pl.ds(k * half, half)
        return remote(
            summed.at[1 - parity, at], pair_in.at[at], pair_send.at[k], pair_recv.at[k], mate
        )

    def chip_copy(target, d):
        return remote(
            paired.at[target], summed_in.at[d], chip_send.at[d], chip_recv.at[d],
            (target * 2 + parity) * 2 + core,
        )

    def pass_on(k):
        core_copy(k).wait()
        for n in range(owners // 2):
            h = k * (owners // 2) + n
            summed[n % 2, k * half + n // 2] = (
                part[core, h].astype(F32) + part_in[h].astype(F32)
            ).astype(BF16)
        pair_copy(k).start()

    def send_far(k):
        pair_copy(k).wait()
        for n in range(half):
            q = k * half + n
            paired[q] = (summed[parity, q].astype(F32) + pair_in[q].astype(F32)).astype(BF16)

            @pl.when(q != pair)
            def _():
                chip_copy(q, lax.rem(q - pair + pairs, pairs)).start()

    @pl.loop(0, blocks)
    def _(i):
        k = block_at(i, me)
        cols = lanes(k)
        mid_copy(k).wait()
        halo_next(k).wait_recv()
        halo_prev(k).wait_recv()
        source = ext[k]
        taps[k, :, 0:LANES] = ext[k, ROW : ROW + tile, :]
        for j in range(1, taps_n):
            taps[k, :, j * LANES : (j + 1) * LANES] = dot(
                hot[(j - 1) * tile : j * tile, :], source
            ).astype(BF16)
        pre = dot(taps[k], wide[...])
        square = pre * pre
        scale = 0.7978845608028654
        t = jnp.tanh(scale * pre * (1.0 + 0.044715 * square))
        half = 0.5 * (1.0 + t)
        active = (pre * half).astype(BF16)
        slope = half + 0.5 * pre * (1.0 - t * t) * scale * (1.0 + 3 * 0.044715 * square)
        gpre[k] = (ups[k] * slope).astype(BF16)
        local = dot(active, cot_ref[...], ((0,), (0,))).astype(BF16)
        for n in range(owners):
            part[n % 2, k * (owners // 2) + n // 2] = local[n * share : (n + 1) * share, :]
        core_copy(k).start()

        g = gpre[k]
        for j in range(1, taps_n):
            terms[(j - 1) * tile : j * tile, :] = dot(
                g, wide_t[:, j * LANES : (j + 1) * LANES]
            ).astype(BF16)
        edges[0, k] = dot(hot_t[0:ROW, :], terms[...]).astype(BF16)
        edge_prev(k).start()
        edges[1, k] = dot(hot_t[ROW + tile :, :], terms[...]).astype(BF16)
        edge_next(k).start()
        pass_on(k)

        @pl.when(i > 0)
        def _():
            send_far(block_at(i - 1, me))

        own = dot(g, wide_t[:, 0:LANES]) + cot_ref[:, cols].astype(F32)
        spread_mid[k] = own + dot(hot_t[ROW : ROW + tile, :], terms[...])
        conv_acc[...] += dot(g, taps[k], ((0,), (0,)))

    send_far(block_at(blocks - 1, me))

    rows_same = lax.broadcasted_iota(jnp.int32, (LANES, LANES), 0) // channels
    cols_same = lax.broadcasted_iota(jnp.int32, (LANES, LANES), 1) // channels
    out_lane = lax.broadcasted_iota(jnp.int32, (LANES, 128), 1)
    in_place = lax.broadcasted_iota(jnp.int32, (LANES, 128), 0) % channels
    total = jnp.zeros((channels, 128), F32)
    for j in range(taps_n):
        block = jnp.where(rows_same == cols_same, conv_acc[:, j * LANES : (j + 1) * LANES], 0.0)
        folded = block[0:channels, :]
        for l in range(1, LANES // channels):
            folded = folded + block[l * channels : (l + 1) * channels, :]
        place = (out_lane == in_place + j * channels).astype(F32)
        total = total + dot(folded, place, precision=lax.Precision.HIGHEST)
    conv_own[...] = total

    def conv_copy(d):
        return remote(
            conv_own, conv_in.at[d], conv_send.at[d], conv_recv.at[d], lax.rem(me + d, devices)
        )

    @pl.loop(1, devices)
    def _(d):
        conv_copy(d).start()

    @pl.loop(0, blocks)
    def _(i):
        k = block_at(i, me)
        edge_prev(k).wait_recv()
        edge_next(k).wait_recv()
        spread_mid[k, 0:ROW, :] += edges_in[1, k].astype(F32)
        spread_mid[k, tile - ROW :, :] += edges_in[0, k].astype(F32)
        grad_ref[:, lanes(k)] = spread_mid[k].astype(BF16)

    conv_in[0] = conv_own[...]

    @pl.loop(1, devices)
    def _(d):
        conv_copy(d).wait()

    def add_conv(owner, acc):
        return acc + conv_in[lax.rem(me - owner + devices, devices)]

    gconv_ref[...] = lax.fori_loop(0, devices, add_conv, jnp.zeros((channels, 128), F32)) * (
        1.0 / (devices * tile * (features // channels)) ** 0.5
    )

    gmix_ref[...] = summed[parity, pair].astype(F32) + pair_in[pair].astype(F32)

    @pl.loop(1, pairs)
    def _(d):
        chip_copy(lax.rem(pair + d, pairs), d).wait()
        gmix_ref[...] += summed_in[d].astype(F32)

    gmix_ref[...] = gmix_ref[...] * (1.0 / (devices * tile) ** 0.5)

    @pl.loop(0, blocks)
    def _(k):
        halo_next(k).wait_send()
        halo_prev(k).wait_send()
        edge_prev(k).wait_send()
        edge_next(k).wait_send()


def shards(columns_in, cotangent, conv_weight, mix_weight, neighbours, rotations, pentagons):
    tile, features = columns_in.shape
    taps_n, channels, _ = conv_weight.shape
    devices = lax.axis_size("space")
    share = features // devices
    chips = devices // 2
    blocks = features // LANES
    width = tile + 2 * ROW

    vmem = pl.BlockSpec(memory_space=pltpu.VMEM)
    grad_input, grad_mix, conv = pl.pallas_call(
        functools.partial(kernel, devices),
        out_shape=(
            jax.ShapeDtypeStruct((tile, features), BF16),
            jax.ShapeDtypeStruct((share, features), F32),
            jax.ShapeDtypeStruct((channels, 128), F32),
        ),
        in_specs=[pl.BlockSpec(memory_space=pltpu.HBM)] * 7,
        out_specs=(vmem,) * 3,
        scratch_shapes=[
            pltpu.VMEM((tile, features), BF16),
            pltpu.VMEM((taps_n, channels, channels), BF16),
            pltpu.VMEM((features, features), BF16),
            pltpu.VMEM((taps_n, tile), jnp.int32),
            pltpu.VMEM((1, tile), jnp.int32),
            pltpu.VMEM((1, tile), jnp.int32),
            pltpu.VMEM((128, tile), jnp.int32),
            pltpu.VMEM((blocks, width, LANES), BF16),
            pltpu.VMEM(((taps_n - 1) * tile, width), BF16),
            pltpu.VMEM((width, (taps_n - 1) * tile), BF16),
            pltpu.VMEM((taps_n * LANES, LANES), BF16),
            pltpu.VMEM((LANES, taps_n * LANES), BF16),
            pltpu.VMEM((blocks, tile, LANES), F32),
            pltpu.VMEM((blocks, tile, taps_n * LANES), BF16),
            pltpu.VMEM((blocks, tile, LANES), BF16),
            pltpu.VMEM(((taps_n - 1) * tile, LANES), BF16),
            pltpu.VMEM((blocks, tile, LANES), F32),
            pltpu.VMEM((2, blocks, ROW, LANES), BF16),
            pltpu.VMEM((2, blocks, ROW, LANES), BF16),
            pltpu.VMEM((2, chips, share, features), BF16),
            pltpu.VMEM((chips, share, features), BF16),
            pltpu.VMEM((2, chips // 2, share, features), BF16),
            pltpu.VMEM((chips // 2, share, features), BF16),
            pltpu.VMEM((chips // 2, share, features), BF16),
            pltpu.VMEM((chips // 2, share, features), BF16),
            pltpu.VMEM((LANES, taps_n * LANES), F32),
            pltpu.VMEM((channels, 128), F32),
            pltpu.VMEM((devices, channels, 128), F32),
            pltpu.SemaphoreType.DMA((6,)),
            pltpu.SemaphoreType.DMA((blocks,)),
            pltpu.SemaphoreType.DMA((2, blocks)),
            pltpu.SemaphoreType.DMA((2, blocks)),
            pltpu.SemaphoreType.DMA((2, blocks)),
            pltpu.SemaphoreType.DMA((2, blocks)),
            pltpu.SemaphoreType.DMA((blocks,)),
            pltpu.SemaphoreType.DMA((blocks,)),
            pltpu.SemaphoreType.DMA((blocks,)),
            pltpu.SemaphoreType.DMA((blocks,)),
            pltpu.SemaphoreType.DMA((chips // 2,)),
            pltpu.SemaphoreType.DMA((chips // 2,)),
            pltpu.SemaphoreType.DMA((devices,)),
            pltpu.SemaphoreType.DMA((devices,)),
        ],
        compiler_params=pltpu.CompilerParams(
            collective_id=0, has_side_effects=True, vmem_limit_bytes=63 * 1024 * 1024
        ),
    )(
        columns_in, cotangent, conv_weight, mix_weight, neighbours.T,
        rotations.reshape(1, tile), pentagons.reshape(1, tile),
    )
    grad_conv = conv.reshape(channels, 128 // channels, channels)[:, :taps_n].transpose(1, 2, 0)
    return grad_input, grad_mix, grad_conv


def solution(mesh):
    return jax.shard_map(
        shards,
        mesh=mesh,
        in_specs=(
            P(("group", "space"), None),
            P(("group", "space"), None),
            P(),
            P(),
            P("space", None),
            P("space"),
            P("space"),
        ),
        out_specs=(P(("group", "space"), None), P("space", "group"), P("group", None, None)),
        check_vma=False,
    )
```
